32 devices in a mesh: seq: 16 (over z, y, core), tab: 2 (over x).
Axes of the slice: x: 2, y: 2, z: 4, core: 2. Of those that a mesh axis runs over, the one named last changes fastest.
Arguments:
- cotangent: bfloat16 [16384, 2560], P('seq', 'tab'), may hold values from -6 to 6
- saved_value: bfloat16 [16384, 2560], P('seq', 'tab'), may hold values from -6 to 6
- gate_scale: float32 [16384], P('seq'), may hold values from 0.2 to 1
- conv_weight: float32 [4, 2560], P(None, 'tab'), may hold values from -3 to 3
- value_weight: bfloat16 [1280, 2560], P(None, 'tab'), may hold values from -0.25 to 0.25
- owner_ids: int32 [8, 16384, 1], P('tab', 'seq'), may hold values from 0 to 15; in each aligned block of 1024 rows (0 to 1023, 1024 to 2047, ..., all dimensions but the last counted through in order) at most 256 rows name the same one
- local_row: int32 [8, 16384], P('tab', 'seq'), may hold values from 0 to 511
- row_table: float32 [8, 8192, 160], P('tab', 'seq'), may hold values from -6 to 6
- moment_one: float32 [8, 8192, 160], P('tab', 'seq'), may hold values from -6 to 6
- moment_two: float32 [8, 8192, 160], P('tab', 'seq'), may hold values from 0.5 to 4
Outputs:
- new_table: float32 [8, 8192, 160], P('tab', 'seq')
- new_first: float32 [8, 8192, 160], P('tab', 'seq')
- new_second: float32 [8, 8192, 160], P('tab', 'seq')
The draws below stay inside these ranges and needn't reach their ends.
Inputs may be any that keep to these rules, and one draw needn't show every extreme that they name: `owner_ids`: within each aligned block of 1024 tokens of one head (one device's tokens), no owner is named by more than 256 tokens; in some blocks one owner is named by exactly 256.
All inputs are finite; a program needn't handle non-finite values.
Results may differ from the reference program's by a relative error of at most 0.0029.
Values may be sent and summed in bfloat16 or wider, within the bound.
A program may use at most 128 MiB of HBM per device.

```python
import math
import jax
import jax.numpy as jnp
import numpy as np

D = 2560
HEADS = 8
HEAD_DIM = 160
TOK_DEV = 1024
ROWS_OWN = 512
MEM = 1280
TOKENS = 16384
ROWS = 8192
CAP = 256
N_SEQ = 16


def with_ends(values, own_key, smallest, largest):
    longest = values.shape.index(max(values.shape))
    spots = []
    for shift in (0, 1):
        where = [jax.random.randint(jax.random.fold_in(own_key, axis), (), 0, length) for axis, length in enumerate(values.shape)]
        where[longest] = (where[longest] + shift) % values.shape[longest]
        spots.append(tuple(where))
    return values.at[spots[0]].set(smallest).at[spots[1]].set(largest)


def spiked(array, key, source, target, shards_of, factor):
    owner, partner = [(jnp.arange(array.shape[axis_at]) // (array.shape[axis_at] // shards_of)).reshape([-1 if axis == axis_at else 1 for axis in range(array.ndim)]) for axis_at in (source, target)]
    chosen = jax.random.permutation(key, shards_of)[partner]
    strong = (owner == chosen) | (owner == (partner + shards_of // 2) % shards_of)
    return jnp.where(strong, factor * array, array)


def shard_levels(key, dims, shards, least, largest):
    gain, own = 1.0, jax.random.fold_in(key, 6)
    for position, shards_of in shards:
        steps = jnp.exp(jax.random.uniform(jax.random.fold_in(own, position), (shards_of,), jnp.float32, least / len(shards), largest / len(shards)))
        gain = gain * jnp.repeat(steps, dims[position] // shards_of).reshape([-1 if axis == position else 1 for axis in range(len(dims))])
    return gain


def rank_table(number_of, slope):
    portions = [(1 << 20) // math.isqrt(rank ** slope) + 1 for rank in range(1, number_of + 1)]
    width = 1 + sum(portions) // (1 << 30)
    return np.cumsum(np.array([max(1, weight // width) for weight in portions]))


def skewed_ids(rng, dims, count, skew):
    grid = rank_table(count, skew)
    lot = jax.random.randint(jax.random.fold_in(rng, 1), dims, 0, int(grid[count - 1]))
    rank = jnp.searchsorted(jnp.asarray(grid, jnp.int32), lot, side="right")
    return jax.random.permutation(jax.random.fold_in(rng, 2), count)[rank].astype(jnp.int32)


def assign_block(key, own, number, rows, count, top, bound, slope):
    order = jax.random.permutation(key, count)
    heavy_load, usual = portions_of(count, rows * top, bound, slope, True), portions_of(count, rows * top, bound, slope, False)
    places = jnp.arange(count)

    def named(lengths, offset_by):
        used = int((lengths > 0).sum())
        fixed = max(1, used // 4)
        shifted = fixed + (places - fixed + offset_by * (used - fixed)) % max(1, count - fixed)
        return jnp.zeros((count,), jnp.int32).at[order[jnp.where(places < fixed, places, shifted)]].set(jnp.asarray(lengths, jnp.int32))

    lengths = jnp.where(number % 4 == 0, named(heavy_load, number // 4), named(usual, number - number // 4 - 1))
    mixed = jax.random.permutation(jax.random.fold_in(own, 3), count)
    giver, sink = mixed[0:count // 2 * 2:2], mixed[1:count // 2 * 2:2]
    room = jnp.minimum(lengths[giver] - 1, bound - lengths[sink]) // 2
    room = jnp.where((giver == order[0]) | (sink == order[0]) | (lengths[sink] == 0), 0, jnp.maximum(room, 0))
    shifted = jax.random.randint(jax.random.fold_in(own, 4), (count // 2,), 0, 1 << 20) % (room + 1)
    lengths = lengths.at[giver].add(-shifted).at[sink].add(shifted)
    labels = jnp.searchsorted(jnp.cumsum(lengths), jnp.arange(rows * top), side="right").astype(jnp.int32)
    grid = labels.reshape(top, rows).T
    grid = grid[jax.random.permutation(jax.random.fold_in(own, 1), rows)]
    offset_by = jax.random.randint(jax.random.fold_in(own, 2), (rows, 1), 0, top)
    return jnp.take_along_axis(grid, (jnp.arange(top)[None, :] + offset_by) % top, axis=1)


def portions_of(number_of, total, bound, lean, full):
    loads = [(1 << 20) // math.isqrt(standing ** lean) + 1 for standing in range(1, number_of + 1)]
    largest = bound if full else min(bound, max(-(-total // number_of), total * loads[0] // sum(loads)))
    least = 1 if total - largest >= number_of - 1 else 0
    given, rest = [largest] + [least] * (number_of - 1), total - largest - least * (number_of - 1)
    while rest > 0:
        movable = [i for i in range(1, number_of) if given[i] < largest] or [i for i in range(1, number_of) if given[i] < bound]
        pool, budget = sum([loads[i] for i in movable]), rest
        for i in movable:
            extra = min(bound - given[i], max(1, budget * loads[i] // pool), rest)
            given[i] = given[i] + extra
            rest = rest - extra
    return np.array(given)


def normal_values(own_key, extent, width, most, split=(), held_as=jnp.bfloat16):
    result = jax.random.normal(own_key, extent, jnp.float32) * width
    if len(split) > 0:
        result = shard_levels(own_key, extent, split, -0.22, 0.18) * result
    return jnp.clip(result, min=-most, max=most).astype(held_as)


def bell_draw_with(own_key, shape, deviation, reach, shards, heavy, kind=jnp.bfloat16):
    entries = deviation * jax.random.normal(own_key, shape, jnp.float32)
    if shards:
        entries = entries * shard_levels(own_key, shape, shards, -0.22, 0.18)
    return jnp.clip(spiked(entries, jax.random.fold_in(own_key, 3), *heavy), -reach, reach).astype(kind)


def setup_inputs(seed: int = 0) -> dict:
    arg_keys = jax.random.split(jax.random.key(seed), 11)
    cotangent = normal_values(arg_keys[0], (TOKENS, D), 1.0, 6.0, ((0, 16), (1, 2)))
    saved_value = normal_values(arg_keys[1], (TOKENS, D), 1.0, 6.0, ((0, 16), (1, 2)))
    gate_scale = jnp.clip(0.2 + 0.8 * jax.random.uniform(arg_keys[2], (TOKENS,), jnp.float32) ** shard_levels(arg_keys[2], (TOKENS,), ((0, 16),), -0.2, 0.2), 0.2, 1.0)
    conv_weight = normal_values(arg_keys[3], (4, D), 0.5, 3.0, ((1, 2),), jnp.float32)
    value_weight = bell_draw_with(arg_keys[4], (MEM, D), MEM ** -0.5, 0.25, ((1, 2),), (1, 0, 2, 2.0))
    owner_ids_keys = jax.random.split(jax.random.fold_in(arg_keys[5], 1), HEADS * TOKENS // TOK_DEV)
    owner_ids_turns = jax.random.permutation(jax.random.fold_in(arg_keys[5], 3), HEADS * TOKENS // TOK_DEV)
    owner_ids = jax.vmap(lambda own, number: assign_block(jax.random.fold_in(arg_keys[5], 2), own, number, TOK_DEV, N_SEQ, 1, CAP, 2))(owner_ids_keys, owner_ids_turns).reshape((HEADS, TOKENS, 1))
    local_row = with_ends(skewed_ids(arg_keys[6], (HEADS, TOKENS), ROWS_OWN, 2), jax.random.fold_in(arg_keys[6], 3), 0, ROWS_OWN - 1).astype(jnp.int32)
    row_table = normal_values(arg_keys[7], (HEADS, ROWS, HEAD_DIM), 1.0, 6.0, ((0, 2), (1, 16)), jnp.float32)
    moment_one = normal_values(arg_keys[8], (HEADS, ROWS, HEAD_DIM), 1.0, 6.0, ((0, 2), (1, 16)), jnp.float32)
    moment_two = jnp.clip(jnp.exp(math.log(4.0) - 2.0794415 * jax.random.uniform(arg_keys[9], (HEADS, ROWS, HEAD_DIM), jnp.float32) ** shard_levels(arg_keys[9], (HEADS, ROWS, HEAD_DIM), ((0, 2), (1, 16)), -0.2, 0.2)), 0.5, 4.0)
    return dict(cotangent=cotangent, saved_value=saved_value, gate_scale=gate_scale, conv_weight=conv_weight, value_weight=value_weight, owner_ids=owner_ids, local_row=local_row, row_table=row_table, moment_one=moment_one, moment_two=moment_two)


beta_one = 0.9
beta_two = 0.95
learn_rate = 0.01
adam_steps = 10.0
epsilon = 1e-08

def reference(cotangent, saved_value, gate_scale, conv_weight, value_weight, owner_ids, local_row, row_table, moment_one, moment_two):
    tokens = cotangent.shape[0]
    upstream = cotangent.astype(jnp.float32)
    value_rows = saved_value.astype(jnp.float32)
    padded_value = jnp.pad(value_rows, ((9, 0), (0, 0)))
    mixed_conv = jnp.zeros(upstream.shape, jnp.float32)
    for tap_index in range(4):
        row_start = 9 - 3 * tap_index
        mixed_conv = mixed_conv + conv_weight[tap_index][None, :] * padded_value[row_start:row_start + tokens]
    squashed = jax.nn.sigmoid(mixed_conv)
    conv_grad = upstream * squashed * (1.0 + mixed_conv * (1.0 - squashed))
    padded_grad = jnp.pad(conv_grad, ((0, 9), (0, 0)))
    value_grad = upstream
    for tap_index in range(4):
        row_start = 3 * tap_index
        value_grad = value_grad + conv_weight[tap_index][None, :] * padded_grad[row_start:row_start + tokens]
    scaled = (gate_scale[:, None] * value_grad).astype(jnp.bfloat16)
    memory_grad = jnp.dot(scaled, value_weight.T, preferred_element_type=jnp.float32)
    heads_grad = jnp.transpose(memory_grad.reshape(tokens, HEADS, HEAD_DIM), (1, 0, 2))
    row_ids = (owner_ids[:, :, 0] * ROWS_OWN + local_row).astype(jnp.int32)
    head_ids = jnp.broadcast_to(jnp.arange(HEADS, dtype=jnp.int32)[:, None], row_ids.shape)
    row_grad = jnp.zeros(row_table.shape, jnp.float32).at[head_ids, row_ids].add(heads_grad)
    row_hits = jnp.zeros(row_table.shape[:2], jnp.int32).at[head_ids, row_ids].add(1)
    touched = (row_hits > 0)[:, :, None]
    first_next = beta_one * moment_one + (1.0 - beta_one) * row_grad
    second_next = beta_two * moment_two + (1.0 - beta_two) * row_grad * row_grad
    update = first_next / (1.0 - beta_one ** adam_steps) / (jnp.sqrt(second_next / (1.0 - beta_two ** adam_steps)) + epsilon)
    table_next = row_table - learn_rate * update
    return (jnp.where(touched, table_next, row_table), jnp.where(touched, first_next, moment_one), jnp.where(touched, second_next, moment_two))
```

```python
import functools

import jax
import jax.numpy as jnp
from jax import lax
from jax.experimental import pallas as pl
from jax.experimental.pallas import tpu as pltpu
from jax.sharding import PartitionSpec as P

beta_one = 0.9
beta_two = 0.95
learn_rate = 0.01
adam_steps = 10.0
epsilon = 1e-08
HALO = 16
GROUP = 4
ROWS_TILE = 128
LANES = 128
CONTRACT_LAST = (((1,), (1,)), ((), ()))


def shifted(block, axis, distance):
    devices = range(lax.axis_size(axis))
    return lax.ppermute(block, axis, [(i, i + distance) for i in devices if i + distance in devices])


def flipped(block, axis, bit):
    return lax.ppermute(block, axis, [(i, i ^ bit) for i in range(lax.axis_size(axis))])


def project_kernel(
    heads, tabs, me_ref, cot_ref, sv_ref, prior_ref, next_cot_ref, next_sv_ref, gate_ref, taps_ref, w_ref, *rest
):
    own_refs, send_refs = rest[:heads], rest[heads : heads * tabs]
    cot_ext, sv_ext, scaled = rest[heads * tabs :]
    step = pl.program_id(0)
    length, width = cot_ref.shape
    f32 = jnp.float32
    sv_ext[:HALO] = prior_ref[...].astype(f32)
    sv_ext[HALO : HALO + length] = sv_ref[...].astype(f32)
    sv_ext[HALO + length :] = next_sv_ref[...].astype(f32)
    cot_ext[:length] = cot_ref[...].astype(f32)
    cot_ext[length:] = next_cot_ref[...].astype(f32)

    for lane in range(0, width, LANES):
        lanes = pl.ds(lane, LANES)
        taps = [taps_ref[k : k + 1, lanes] for k in range(4)]

        @pl.loop(0, length // ROWS_TILE)
        def _(tile):
            start = pl.multiple_of(tile * ROWS_TILE, ROWS_TILE)
            reach = ROWS_TILE + HALO
            context = sv_ext[pl.ds(start, reach + HALO), lanes]
            upstream = cot_ext[pl.ds(start, reach), lanes]
            mixed = taps[0] * context[HALO:]
            for k in range(1, 4):
                mixed = mixed + taps[k] * context[HALO - 3 * k : HALO - 3 * k + reach]
            squashed = 1.0 / (1.0 + jnp.exp(-mixed))
            grad = upstream * squashed * (1.0 + mixed * (1.0 - squashed))
            total = upstream[:ROWS_TILE]
            for k in range(4):
                total = total + taps[k] * grad[3 * k : 3 * k + ROWS_TILE]
            total = gate_ref[pl.ds(start, ROWS_TILE), :] * total
            column = pl.multiple_of(step * width + lane, LANES)
            scaled[pl.ds(start, ROWS_TILE), pl.ds(column, LANES)] = total.astype(jnp.bfloat16)

    @pl.when(step == pl.num_programs(0) - 1)
    def _():
        head_dim = own_refs[0].shape[0]
        for away in range(tabs):
            owner = lax.rem(me_ref[0] + away, tabs)
            for head in range(heads):
                first = pl.multiple_of((owner * heads + head) * head_dim, 32)
                part = lax.dot_general(
                    w_ref[pl.ds(first, head_dim), :], scaled[...], CONTRACT_LAST, preferred_element_type=f32
                )
                if away == 0:
                    own_refs[head][...] = part
                else:
                    send_refs[(away - 1) * heads + head][...] = part.astype(jnp.bfloat16)


def project(cotangent, saved_value, prior, next_cot, next_sv, gate, taps, weight, heads, tabs):
    length, features = cotangent.shape
    memory = weight.shape[0]
    head_dim = memory // (heads * tabs)
    width = next(w for w in (256, 128, features) if features % w == 0)
    own = [jax.ShapeDtypeStruct((head_dim, length), jnp.float32)] * heads
    send = [jax.ShapeDtypeStruct((head_dim, length), jnp.bfloat16)] * (heads * (tabs - 1))
    feature_block = lambda rows: pl.BlockSpec((rows, width), lambda i, me: (0, i))
    whole = lambda shape: pl.BlockSpec(shape, lambda i, me: (0, 0))
    outs = pl.pallas_call(
        functools.partial(project_kernel, heads, tabs),
        out_shape=own + send,
        grid_spec=pltpu.PrefetchScalarGridSpec(
            num_scalar_prefetch=1,
            grid=(features // width,),
            in_specs=[
                feature_block(length),
                feature_block(length),
                feature_block(HALO),
                feature_block(HALO),
                feature_block(HALO),
                whole((length, 1)),
                feature_block(4),
                whole(weight.shape),
            ],
            out_specs=[whole((head_dim, length))] * (heads * tabs),
            scratch_shapes=[
                pltpu.VMEM((length + HALO, width), jnp.float32),
                pltpu.VMEM((length + 2 * HALO, width), jnp.float32),
                pltpu.VMEM((length, features), jnp.bfloat16),
            ],
        ),
        compiler_params=pltpu.CompilerParams(vmem_limit_bytes=48 * 1024 * 1024),
        cost_estimate=pl.CostEstimate(
            flops=2 * length * features * memory, bytes_accessed=16 * 1024 * 1024, transcendentals=length * features
        ),
    )(lax.axis_index("tab")[None].astype(jnp.int32), cotangent, saved_value, prior, next_cot, next_sv, gate, taps, weight)
    return outs[:heads], [outs[heads * k : heads * (k + 1)] for k in range(1, tabs)]


def exchange_kernel(heads, tabs, planes, *refs):
    own_refs, send_refs = refs[:heads], refs[heads : heads * tabs]
    place_ref, sums_ref, hits_ref = refs[heads * tabs : heads * tabs + 3]
    (
        tab_in, mine, core_in, side_in, diag_in, table_out, table_in, count_out, count_in,
        tab_sems, core_sems, side_sems, diag_sems, table_sems, count_sems,
    ) = refs[heads * tabs + 3 :]
    head_dim, length = own_refs[0].shape
    rows = sums_ref.shape[2]
    seq, tab = lax.axis_index("seq"), lax.axis_index("tab")
    plane, column = seq // GROUP, seq % GROUP
    core = seq + 1 - 2 * (seq % 2)
    side = seq + 2 - 4 * ((seq // 2) % 2)
    tab_peer = lambda k: lax.rem(tab + k, tabs)
    plane_peer = lambda k: lax.rem(plane + k, planes) * GROUP + column

    count_out[...] = jnp.zeros_like(count_out)
    barrier = pltpu.get_barrier_semaphore()

    def greet(**place):
        pl.semaphore_signal(barrier, inc=1, device_id=place, device_id_type=pl.DeviceIdType.MESH)

    for k in range(1, tabs):
        greet(tab=tab_peer(k))
    greet(seq=core)
    greet(seq=side)
    for k in range(1, planes):
        greet(seq=plane_peer(k))
    pl.semaphore_wait(barrier, tabs + planes)

    def copy(source, target, sems, place):
        return pltpu.make_async_remote_copy(
            src_ref=source,
            dst_ref=target,
            send_sem=sems.at[0],
            recv_sem=sems.at[1],
            device_id=place,
            device_id_type=pl.DeviceIdType.MESH,
        )

    tab_copy = lambda k, h: copy(
        send_refs[(k - 1) * heads + h], tab_in.at[k - 1, h], tab_sems.at[k - 1, h], {"tab": tab_peer(k)}
    )
    core_copy = lambda h: copy(mine.at[h], core_in.at[h], core_sems.at[h], {"seq": core})
    side_copy = lambda h: copy(mine.at[h], side_in.at[h], side_sems.at[h], {"seq": side})
    diag_copy = lambda h: copy(side_in.at[h], diag_in.at[h], diag_sems.at[h], {"seq": core})
    table_copy = lambda k, h: copy(
        table_out.at[h, k - 1], table_in.at[h, k - 1], table_sems.at[h, k - 1], {"seq": plane_peer(k)}
    )
    count_copy = lambda k: copy(count_out.at[k], count_in.at[k - 1], count_sems.at[k - 1], {"seq": plane_peer(k)})

    for h in range(heads):
        for k in range(1, tabs):
            tab_copy(k, h).start()

    def combine(h):
        total = own_refs[h][...]
        for k in range(1, tabs):
            tab_copy(k, h).wait_recv()
            total = total + tab_in[k - 1, h].astype(jnp.float32)
        mine[h] = total.astype(jnp.bfloat16)
        side_copy(h).start()
        core_copy(h).start()

    def forward(h):
        side_copy(h).wait_recv()
        diag_copy(h).start()

    def add_up(h):
        core_copy(h).wait_recv()
        diag_copy(h).wait_recv()
        row = lax.broadcasted_iota(jnp.int32, (rows, length), 0)
        ones = jnp.ones((16, length), jnp.bfloat16)

        def sums_of(away):
            total = jnp.zeros((head_dim + 16, rows), jnp.float32)
            for source, held in enumerate((mine, core_in, side_in, diag_in)):
                place = place_ref[h * GROUP + source : h * GROUP + source + 1, :] - away * rows
                chosen = (place == row).astype(jnp.float32).astype(jnp.bfloat16)
                grads = jnp.concatenate([held[h], ones], axis=0)
                total = total + lax.dot_general(grads, chosen, CONTRACT_LAST, preferred_element_type=jnp.float32)
            return total

        @pl.loop(1, planes)
        def _(away):
            total = sums_of(away)
            table_out[h, away - 1] = total[:head_dim].astype(jnp.bfloat16)
            count_out[away, h : h + 1] = total[head_dim : head_dim + 1]
            table_copy(away, h).start()

        total = sums_of(0)
        sums_ref[h] = total[:head_dim]
        count_out[0, h : h + 1] = total[head_dim : head_dim + 1]

    combine(0)
    for h in range(heads):
        if h + 1 < heads:
            combine(h + 1)
        forward(h)
        add_up(h)

    for k in range(1, planes):
        count_copy(k).start()
    for h in range(heads):
        total = sums_ref[h]
        for k in range(1, planes):
            table_copy(k, h).wait_recv()
            total = total + table_in[h, k - 1].astype(jnp.float32)
        sums_ref[h] = total
    counts = count_out[0]
    for k in range(1, planes):
        count_copy(k).wait_recv()
        counts = counts + count_in[k - 1]
    hits_ref[...] = counts
    for h in range(heads):
        for k in range(1, tabs):
            tab_copy(k, h).wait_send()
        side_copy(h).wait_send()
        core_copy(h).wait_send()
        diag_copy(h).wait_send()
        for k in range(1, planes):
            table_copy(k, h).wait_send()
    for k in range(1, planes):
        count_copy(k).wait_send()


def exchange(own, send, places, rows, tabs, planes):
    heads = len(own)
    head_dim, length = own[0].shape
    vmem = pl.BlockSpec(memory_space=pltpu.VMEM)
    block = (head_dim, length)
    count_rows = -(-heads // 8) * 8
    pairs = lambda *shape: pltpu.SemaphoreType.DMA((*shape, 2))
    return pl.pallas_call(
        functools.partial(exchange_kernel, heads, tabs, planes),
        out_shape=[
            jax.ShapeDtypeStruct((heads, head_dim, rows), jnp.float32),
            jax.ShapeDtypeStruct((count_rows, rows), jnp.float32),
        ],
        in_specs=[vmem] * (heads * tabs + 1),
        out_specs=[vmem, vmem],
        scratch_shapes=[
            pltpu.VMEM((max(tabs - 1, 1), heads, *block), jnp.bfloat16),
            pltpu.VMEM((heads, *block), jnp.bfloat16),
            pltpu.VMEM((heads, *block), jnp.bfloat16),
            pltpu.VMEM((heads, *block), jnp.bfloat16),
            pltpu.VMEM((heads, *block), jnp.bfloat16),
            pltpu.VMEM((heads, planes - 1, head_dim, rows), jnp.bfloat16),
            pltpu.VMEM((heads, planes - 1, head_dim, rows), jnp.bfloat16),
            pltpu.VMEM((planes, count_rows, rows), jnp.float32),
            pltpu.VMEM((planes - 1, count_rows, rows), jnp.float32),
            pairs(max(tabs - 1, 1), heads),
            pairs(heads),
            pairs(heads),
            pairs(heads),
            pairs(heads, planes - 1),
            pairs(planes - 1),
        ],
        compiler_params=pltpu.CompilerParams(
            vmem_limit_bytes=52 * 1024 * 1024, collective_id=0, has_side_effects=True
        ),
        cost_estimate=pl.CostEstimate(
            flops=2 * planes * heads * GROUP * length * rows * 256, bytes_accessed=8 * 1024 * 1024, transcendentals=0
        ),
    )(*own, *send, places)


def shards(
    cotangent,
    saved_value,
    gate_scale,
    conv_weight,
    value_weight,
    owner_ids,
    local_row,
    row_table,
    moment_one,
    moment_two,
):
    length = cotangent.shape[0]
    heads, rows, head_dim = row_table.shape
    seqs, tabs = lax.axis_size("seq"), lax.axis_size("tab")
    planes = seqs // GROUP
    me = lax.axis_index("seq")
    plane, column = me // GROUP, me % GROUP

    prior = shifted(saved_value[length - HALO :], "seq", 1)
    next_rows = shifted(jnp.stack([cotangent[:HALO], saved_value[:HALO]]), "seq", -1)

    owners = owner_ids[:, :, 0]
    ids = owners * rows + local_row
    core_ids = flipped(ids, "seq", 1)
    side_ids = flipped(ids, "seq", 2)
    diag_ids = flipped(ids, "seq", 3)
    group_ids = jnp.stack([ids, core_ids, side_ids, diag_ids], axis=1)
    owner = group_ids // rows
    away = (owner // GROUP + planes - plane) % planes
    places = jnp.where(owner % GROUP == column, away * rows + group_ids % rows, -1)

    own, send = project(
        cotangent,
        saved_value,
        prior,
        next_rows[0],
        next_rows[1],
        gate_scale[:, None],
        conv_weight,
        value_weight,
        heads,
        tabs,
    )
    row_grad, hits = exchange(
        own, [part for parts in send for part in parts], places.reshape(heads * GROUP, length), rows, tabs, planes
    )
    touched = (hits[:heads] > 0)[:, None, :]
    turned = lambda array: jnp.swapaxes(array, 1, 2)
    table, first, second = turned(row_table), turned(moment_one), turned(moment_two)
    first_next = beta_one * first + (1.0 - beta_one) * row_grad
    second_next = beta_two * second + (1.0 - beta_two) * row_grad * row_grad
    update = (
        first_next
        / (1.0 - beta_one**adam_steps)
        / (jnp.sqrt(second_next / (1.0 - beta_two**adam_steps)) + epsilon)
    )
    table_next = table - learn_rate * update
    return (
        turned(jnp.where(touched, table_next, table)),
        turned(jnp.where(touched, first_next, first)),
        turned(jnp.where(touched, second_next, second)),
    )


def solution(mesh):
    in_specs = (
        P("seq", "tab"),
        P("seq", "tab"),
        P("seq"),
        P(None, "tab"),
        P(None, "tab"),
        P("tab", "seq", None),
        P("tab", "seq"),
        P("tab", "seq", None),
        P("tab", "seq", None),
        P("tab", "seq", None),
    )
    out_specs = (P("tab", "seq", None), P("tab", "seq", None), P("tab", "seq", None))
    return jax.shard_map(shards, mesh=mesh, in_specs=in_specs, out_specs=out_specs, check_vma=False)
```

```python
import functools

import jax
import jax.numpy as jnp
from jax import lax
from jax.experimental import pallas as pl
from jax.experimental.pallas import tpu as pltpu
from jax.sharding import PartitionSpec as P

beta_one = 0.9
beta_two = 0.95
learn_rate = 0.01
adam_steps = 10.0
epsilon = 1e-08
HALO = 16
GROUP = 4
ROWS_TILE = 128
LANES = 128
CONTRACT_LAST = (((1,), (1,)), ((), ()))


def conv_tile(context, upstream, gate, taps):
    reach, rows = upstream.shape[0], gate.shape[0]
    mixed = taps[0] * context[HALO : HALO + reach]
    for k in range(1, 4):
        mixed = mixed + taps[k] * context[HALO - 3 * k : HALO - 3 * k + reach]
    swing = 0.5 * jnp.tanh(0.5 * mixed)
    grad = upstream * (0.5 + swing) * (1.0 + mixed * (0.5 - swing))
    total = upstream[:rows]
    for k in range(4):
        total = total + taps[k] * grad[3 * k : 3 * k + rows]
    return (gate * total).astype(jnp.bfloat16)


def coded(values):
    peak = jnp.maximum(jnp.max(jnp.abs(values), axis=0, keepdims=True), 1e-30)
    steps = jnp.floor(values * (32766.0 / peak) + 0.5)
    return steps.astype(jnp.int32).astype(jnp.int16), peak * (1.0 / 32766.0)


def decoded(steps, scale):
    return steps.astype(jnp.int32).astype(jnp.float32) * scale


def layer_kernel(heads, tabs, planes, *refs):
    cot_ref, sv_ref, gate_ref, taps_ref, w_hbm, ids_ref, sums_ref, hits_ref = refs[:8]
    (
        w_ref, scaled, halos, ids_in, tab_out, tab_in, mine, core_in, side_in, diag_in, table_out, table_in, relayed,
        tab_scale_out, tab_scale_in, meta_out, meta_in, hit_sums, w_sem, halo_sems, ids_sems, tab_sems, tab_scale_sems,
        core_sems, side_sems, diag_sems, table_sems, meta_sems,
    ) = refs[8:]
    f32 = jnp.float32
    length, features = cot_ref.shape
    head_dim, rows = sums_ref.shape[1:]
    seqs = planes * GROUP
    seq, tab = lax.axis_index("seq"), lax.axis_index("tab")
    plane, column = seq // GROUP, seq % GROUP
    core = seq + 1 - 2 * (seq % 2)
    side = seq + 2 - 4 * ((seq // 2) % 2)
    diag = core + side - seq
    after, before = lax.rem(seq + 1, seqs), lax.rem(seq + seqs - 1, seqs)
    tab_peer = lambda k: lax.rem(tab + k, tabs)
    plane_peer = lambda k: lax.rem(plane + k, planes) * GROUP + column
    relays = planes == 4

    w_copy = pltpu.make_async_copy(w_hbm, w_ref, w_sem)
    w_copy.start()
    hits_ref[...] = jnp.zeros_like(hits_ref)
    barrier = pltpu.get_barrier_semaphore()

    def greet(**place):
        pl.semaphore_signal(barrier, inc=1, device_id=place, device_id_type=pl.DeviceIdType.MESH)

    for k in range(1, tabs):
        greet(tab=tab_peer(k))
    for peer in (core, side, diag, after, before):
        greet(seq=peer)
    for k in range(1, planes):
        greet(seq=plane_peer(k))
    pl.semaphore_wait(barrier, tabs + planes + 3)

    def copy(source, target, sems, place):
        return pltpu.make_async_remote_copy(
            src_ref=source,
            dst_ref=target,
            send_sem=sems.at[0],
            recv_sem=sems.at[1],
            device_id=place,
            device_id_type=pl.DeviceIdType.MESH,
        )

    halo_copies = [
        copy(sv_ref.at[pl.ds(length - HALO, HALO)], halos.at[0], halo_sems.at[0], {"seq": after}),
        copy(cot_ref.at[pl.ds(0, HALO)], halos.at[1], halo_sems.at[1], {"seq": before}),
        copy(sv_ref.at[pl.ds(0, HALO)], halos.at[2], halo_sems.at[2], {"seq": before}),
    ]
    ids_copies = [copy(ids_ref, ids_in.at[i], ids_sems.at[i], {"seq": p}) for i, p in enumerate((core, side, diag))]
    tab_copy = lambda k, h: copy(
        tab_out.at[k - 1, h], tab_in.at[k - 1, h], tab_sems.at[k - 1, h], {"tab": tab_peer(k)}
    )
    core_copy = lambda h: copy(mine.at[h], core_in.at[h], core_sems.at[h], {"seq": core})
    side_copy = lambda h: copy(mine.at[h], side_in.at[h], side_sems.at[h], {"seq": side})
    diag_copy = lambda h: copy(side_in.at[h], diag_in.at[h], diag_sems.at[h], {"seq": core})
    scale_copy = lambda k, h: copy(
        tab_scale_out.at[k - 1, h], tab_scale_in.at[k - 1, h], tab_scale_sems.at[k - 1, h], {"tab": tab_peer(k)}
    )

    def slot_copies(slot, h, target):
        return (
            copy(table_out.at[h, slot], table_in.at[h, slot], table_sems.at[h, slot], {"seq": target}),
            copy(meta_out.at[h, slot], meta_in.at[h, slot], meta_sems.at[h, slot], {"seq": target}),
        )

    def table_copies(k, h):
        return slot_copies(k - 1, h, plane_peer(k))

    def relay_copies(h):
        return slot_copies(1, h, lax.rem(2 * plane + 1, 5) * GROUP + column)

    def send(copies):
        for one in copies:
            one.start()

    def receive(copies):
        for one in copies:
            one.wait_recv()

    def put(h, slot, total, hits):
        table_out[h, slot], meta_out[h, slot, 0:1] = coded(total)
        meta_out[h, slot, 1:2] = hits

    def take(h, slot):
        return decoded(table_in[h, slot], meta_in[h, slot, 0:1]), meta_in[h, slot, 1:2]

    for started in halo_copies + ids_copies:
        started.start()

    tiles = length // ROWS_TILE

    def taps_at(lanes):
        return [taps_ref[k : k + 1, lanes] for k in range(4)]

    @pl.loop(0, features // LANES)
    def _(group):
        lanes = pl.ds(pl.multiple_of(group * LANES, LANES), LANES)
        taps = taps_at(lanes)

        @pl.loop(1, tiles - 1)
        def _(tile):
            start = pl.multiple_of(tile * ROWS_TILE, ROWS_TILE)
            behind = pl.multiple_of(tile * ROWS_TILE - HALO, HALO)
            context = sv_ref[pl.ds(behind, ROWS_TILE + 2 * HALO), lanes].astype(f32)
            upstream = cot_ref[pl.ds(start, ROWS_TILE + HALO), lanes].astype(f32)
            gate = gate_ref[pl.ds(start, ROWS_TILE), :]
            scaled[pl.ds(start, ROWS_TILE), lanes] = conv_tile(context, upstream, gate, taps)

    for arrived in halo_copies:
        arrived.wait()

    @pl.when(seq == 0)
    def _():
        halos[0] = jnp.zeros_like(halos[0])

    @pl.when(seq == seqs - 1)
    def _():
        halos[1] = jnp.zeros_like(halos[1])
        halos[2] = jnp.zeros_like(halos[2])

    @pl.loop(0, features // LANES)
    def _(group):
        lanes = pl.ds(pl.multiple_of(group * LANES, LANES), LANES)
        taps = taps_at(lanes)
        context = jnp.concatenate([halos[0, :, lanes], sv_ref[: ROWS_TILE + HALO, lanes]], axis=0).astype(f32)
        upstream = cot_ref[: ROWS_TILE + HALO, lanes].astype(f32)
        scaled[:ROWS_TILE, lanes] = conv_tile(context, upstream, gate_ref[:ROWS_TILE, :], taps)
        last = length - ROWS_TILE
        context = jnp.concatenate([sv_ref[last - HALO :, lanes], halos[2, :, lanes]], axis=0).astype(f32)
        upstream = jnp.concatenate([cot_ref[last:, lanes], halos[1, :, lanes]], axis=0).astype(f32)
        scaled[last:, lanes] = conv_tile(context, upstream, gate_ref[last:, :], taps)

    w_copy.wait()

    def part(away, h):
        first = pl.multiple_of((tab_peer(away) * heads + h) * head_dim, 32)
        return lax.dot_general(
            w_ref[pl.ds(first, head_dim), :], scaled[...], CONTRACT_LAST, preferred_element_type=f32
        )

    for h in range(heads):
        for k in range(1, tabs):
            tab_out[k - 1, h], tab_scale_out[k - 1, h] = coded(part(k, h))
            tab_copy(k, h).start()
            scale_copy(k, h).start()

    def combine(h):
        total = part(0, h)
        for k in range(1, tabs):
            tab_copy(k, h).wait_recv()
            scale_copy(k, h).wait_recv()
            total = total + decoded(tab_in[k - 1, h], tab_scale_in[k - 1, h])
        mine[h] = total.astype(jnp.bfloat16)
        side_copy(h).start()
        core_copy(h).start()

    def forward(h):
        side_copy(h).wait_recv()
        diag_copy(h).start()

    middle, final = (3 - 2 * (plane // 2), 1 + 2 * (plane // 2)) if relays else (0, 0)
    edge = 1 - ((plane + 1) // 2) % 2

    def add_up(h):
        core_copy(h).wait_recv()
        diag_copy(h).wait_recv()
        row = lax.broadcasted_iota(jnp.int32, (rows, length), 0)
        ones = jnp.ones((16, length), jnp.bfloat16)

        def sums_of(away):
            first = plane_peer(away) * rows
            total = jnp.zeros((head_dim + 16, rows), f32)
            for source, held in enumerate((mine, core_in, side_in, diag_in)):
                ids = ids_ref[h : h + 1, :] if source == 0 else ids_in[source - 1, h : h + 1, :]
                chosen = (ids - first == row).astype(f32).astype(jnp.bfloat16)
                grads = jnp.concatenate([held[h], ones], axis=0)
                total = total + lax.dot_general(grads, chosen, CONTRACT_LAST, preferred_element_type=f32)
            return total[:head_dim], total[head_dim : head_dim + 1]

        if relays:
            put(h, 1, *sums_of(2))
            send(relay_copies(h))
            put(h, middle - 1, *sums_of(middle))
            send(table_copies(middle, h))
            relayed[h], hit_sums[h] = sums_of(final)

            @pl.when(edge == 1)
            def _():
                put(h, final - 1, relayed[h], hit_sums[h])
                send(table_copies(final, h))

        else:

            @pl.loop(1, planes)
            def _(away):
                put(h, away - 1, *sums_of(away))
                send(table_copies(away, h))

        sums_ref[h], hits_ref[h] = sums_of(0)

    def relay(h):
        @pl.when(edge == 0)
        def _():
            receive(relay_copies(h))
            total, hits = take(h, 1)
            put(h, final - 1, relayed[h] + total, hit_sums[h] + hits)
            send(table_copies(final, h))

    def collect(h, slot):
        total, hits = take(h, slot)
        sums_ref[h] = sums_ref[h] + total
        hits_ref[h] = hits_ref[h] + hits

    combine(0)
    for arrived in ids_copies:
        arrived.wait()
    for h in range(heads):
        if h + 1 < heads:
            combine(h + 1)
        forward(h)
        add_up(h)
        if relays and h > 0:
            relay(h - 1)
    if relays:
        relay(heads - 1)

    for h in range(heads):
        if relays:
            for k in (1, 3):
                receive(table_copies(k, h))
                collect(h, k - 1)

            @pl.when(edge == 1)
            def _():
                receive(relay_copies(h))
                collect(h, 1)

        else:
            for k in range(1, planes):
                receive(table_copies(k, h))
                collect(h, k - 1)
    for h in range(heads):
        for k in range(1, tabs):
            tab_copy(k, h).wait_send()
            scale_copy(k, h).wait_send()
        side_copy(h).wait_send()
        core_copy(h).wait_send()
        diag_copy(h).wait_send()
        for k in range(1, planes):
            for one in table_copies(k, h):
                one.wait_send()


def layer(cotangent, saved_value, gate, taps, weight, ids, rows, head_dim, tabs, planes):
    heads, length = ids.shape
    features = cotangent.shape[1]
    vmem = pl.BlockSpec(memory_space=pltpu.VMEM)
    bf16, f32 = jnp.bfloat16, jnp.float32
    block = (heads, head_dim, length)
    tables = (heads, planes - 1, head_dim, rows)
    pairs = lambda *shape: pltpu.SemaphoreType.DMA((*shape, 2))
    return pl.pallas_call(
        functools.partial(layer_kernel, heads, tabs, planes),
        out_shape=[
            jax.ShapeDtypeStruct((heads, head_dim, rows), f32),
            jax.ShapeDtypeStruct((heads, 1, rows), f32),
        ],
        in_specs=[vmem, vmem, vmem, vmem, pl.BlockSpec(memory_space=pl.ANY), vmem],
        out_specs=[vmem, vmem],
        scratch_shapes=[
            pltpu.VMEM(weight.shape, bf16),
            pltpu.VMEM((length, features), bf16),
            pltpu.VMEM((3, HALO, features), bf16),
            pltpu.VMEM((3, heads, length), jnp.int32),
            pltpu.VMEM((max(tabs - 1, 1), *block), jnp.int16),
            pltpu.VMEM((max(tabs - 1, 1), *block), jnp.int16),
            pltpu.VMEM(block, bf16),
            pltpu.VMEM(block, bf16),
            pltpu.VMEM(block, bf16),
            pltpu.VMEM(block, bf16),
            pltpu.VMEM(tables, jnp.int16),
            pltpu.VMEM(tables, jnp.int16),
            pltpu.VMEM((heads, head_dim, rows), f32),
            pltpu.VMEM((max(tabs - 1, 1), heads, 1, length), f32),
            pltpu.VMEM((max(tabs - 1, 1), heads, 1, length), f32),
            pltpu.VMEM((heads, planes - 1, 2, rows), f32),
            pltpu.VMEM((heads, planes - 1, 2, rows), f32),
            pltpu.VMEM((heads, 1, rows), f32),
            pltpu.SemaphoreType.DMA,
            pairs(3),
            pairs(3),
            pairs(max(tabs - 1, 1), heads),
            pairs(max(tabs - 1, 1), heads),
            pairs(heads),
            pairs(heads),
            pairs(heads),
            pairs(heads, planes - 1),
            pairs(heads, planes - 1),
        ],
        compiler_params=pltpu.CompilerParams(
            vmem_limit_bytes=56 * 1024 * 1024, collective_id=0, has_side_effects=True
        ),
    )(cotangent, saved_value, gate, taps, weight, ids)


def shards(
    cotangent,
    saved_value,
    gate_scale,
    conv_weight,
    value_weight,
    owner_ids,
    local_row,
    row_table,
    moment_one,
    moment_two,
):
    heads, rows, head_dim = row_table.shape
    tabs, planes = lax.axis_size("tab"), lax.axis_size("seq") // GROUP
    ids = owner_ids[:, :, 0] * rows + local_row
    row_grad, hits = layer(
        cotangent, saved_value, gate_scale[:, None], conv_weight, value_weight, ids, rows, head_dim, tabs, planes
    )
    touched = hits > 0
    turned = lambda array: jnp.swapaxes(array, 1, 2)
    table, first, second = turned(row_table), turned(moment_one), turned(moment_two)
    first_next = beta_one * first + (1.0 - beta_one) * row_grad
    second_next = beta_two * second + (1.0 - beta_two) * row_grad * row_grad
    update = (
        first_next
        / (1.0 - beta_one**adam_steps)
        / (jnp.sqrt(second_next / (1.0 - beta_two**adam_steps)) + epsilon)
    )
    table_next = table - learn_rate * update
    return (
        turned(jnp.where(touched, table_next, table)),
        turned(jnp.where(touched, first_next, first)),
        turned(jnp.where(touched, second_next, second)),
    )


def solution(mesh):
    in_specs = (
        P("seq", "tab"),
        P("seq", "tab"),
        P("seq"),
        P(None, "tab"),
        P(None, "tab"),
        P("tab", "seq", None),
        P("tab", "seq"),
        P("tab", "seq", None),
        P("tab", "seq", None),
        P("tab", "seq", None),
    )
    out_specs = (P("tab", "seq", None), P("tab", "seq", None), P("tab", "seq", None))
    return jax.shard_map(shards, mesh=mesh, in_specs=in_specs, out_specs=out_specs, check_vma=False)
```
